128 devices in a mesh: pair: 8 (over y, core), slab: 16 (over x, z).
Axes of the slice: x: 4, y: 4, z: 4, core: 2. Of those that a mesh axis runs over, the one named last changes fastest.
Arguments:
- amplitudes: bfloat16 [16, 1536, 1536], P('slab', 'pair'), may hold values from -6 to 6
- integrals: bfloat16 [16, 1536, 1536], P('slab', 'pair'), may hold values from -0.4375 to 0.4375
- occ_slab: int32 [16], P('slab'), may hold values from 0 to 7
- occ_inner: int32 [1], replicated, may hold values from 0 to 7
- occ_outer: int32 [16], replicated, may hold values from 0 to 7
- vir_offset: int32 [9], replicated, may hold values from 0 to 1536, as said below
- residual: bfloat16 [16, 1536, 24576], P('slab', 'pair'), may hold values from -6 to 6
Outputs:
- updated: bfloat16 [16, 1536, 24576], P('slab', 'pair')
The draws below stay inside these ranges and needn't reach their ends.
Inputs may be any that keep to these rules, and one draw needn't show every extreme that they name: vir_offset[0] is 0, vir_offset[8] is 1536, and the entries rise strictly.
All inputs are finite; a program needn't handle non-finite values.
Results may differ from the reference program's by a relative error of at most 0.001.
Values may be sent and summed in bfloat16 or wider, within the bound.
No kernel may reach another device: no remote copies, remote signals or barrier semaphores. Data moves between devices by JAX's collectives and lax.ppermute only.
A program may use at most 128 MiB of HBM per device.

```python
import jax
import jax.numpy as jnp
from jax import lax

V = 1536
M = 1
I = 16
J = 16


def draw_vir_offset(key, part):
    key = jax.random.fold_in(key, 7)
    cuts = jax.random.permutation(key, V - 1)[:7] + 1
    cuts = jnp.sort(cuts).astype(jnp.int32)
    return jnp.concatenate([jnp.zeros((1,), jnp.int32), cuts, jnp.full((1,), V, jnp.int32)])


def plant(values, key, smallest, high):
    extent = values.shape
    place = [jax.random.randint(jax.random.fold_in(key, axis), (), 0, extent[axis]) for axis in range(len(extent))]
    values = values.at[tuple(place)].set(smallest)
    longest = extent.index(max(extent))
    place[longest] = (place[longest] + 1) % extent[longest]
    return values.at[tuple(place)].set(high)


def block_scale(rng, extent, split, least, top_value):
    factor_of, own = 1.0, jax.random.fold_in(rng, 6)
    for axis_at, shards_of in split:
        draws = jnp.exp(jax.random.uniform(jax.random.fold_in(own, axis_at), (shards_of,), jnp.float32, least / len(split), top_value / len(split)))
        factor_of = factor_of * jnp.repeat(draws, extent[axis_at] // shards_of).reshape([-1 if axis == axis_at else 1 for axis in range(len(extent))])
    return factor_of


def noise(own_key, extent, spread, limit, split=(), kind=jnp.bfloat16):
    values = jax.random.normal(own_key, extent, jnp.float32) * spread
    if len(split) > 0:
        values = block_scale(own_key, extent, split, -0.22, 0.18) * values
    return jnp.clip(values, min=-limit, max=limit).astype(kind)


def setup_inputs(seed: int = 0) -> dict:
    keys = jax.random.split(jax.random.key(seed), 8)
    amplitudes = noise(keys[0], (I, V, M * V), 1.0, 6.0, ((0, 16), (1, 8)))
    integrals = noise(keys[1], (J, V, M * V), (M * V // 8) ** -0.5, 0.4375, ((0, 16), (1, 8)))
    occ_slab = plant(jax.random.randint(keys[2], (I,), 0, 8), jax.random.fold_in(keys[2], 1), 0, 7).astype(jnp.int32)
    occ_inner = jax.random.randint(keys[3], (M,), 0, 8).astype(jnp.int32)
    occ_outer = plant(jax.random.randint(keys[4], (J,), 0, 8), jax.random.fold_in(keys[4], 1), 0, 7).astype(jnp.int32)
    vir_offset = draw_vir_offset(jax.random.fold_in(keys[7], 71), 0)
    residual = noise(keys[6], (I, V, J * V), 1.0, 6.0, ((0, 16), (1, 8)))
    return {"amplitudes": amplitudes, "integrals": integrals, "occ_slab": occ_slab, "occ_inner": occ_inner, "occ_outer": occ_outer, "vir_offset": vir_offset, "residual": residual}


def vir_labels(vir_offset):
    position = jnp.arange(V, dtype=jnp.int32)
    return jnp.sum((position[:, None] >= vir_offset[None, 1:8]).astype(jnp.int32), axis=1).astype(jnp.int32)


def reference(amplitudes, integrals, occ_slab, occ_inner, occ_outer, vir_offset, residual):
    labels = vir_labels(vir_offset)
    k_labels = jnp.bitwise_xor(occ_inner[:, None], labels[None, :]).reshape(-1)
    wmask = jnp.bitwise_xor(
        jnp.bitwise_xor(occ_outer[:, None, None], labels[None, :, None]), k_labels[None, None, :]) == 0
    int_wide = (integrals * wmask.astype(integrals.dtype)).astype(jnp.float32)

    def one_row(inputs):
        amp_row, label_row, res_row = inputs
        amask = jnp.bitwise_xor(jnp.bitwise_xor(label_row, labels[:, None]), k_labels[None, :]) == 0
        amp_wide = (amp_row * amask.astype(amp_row.dtype)).astype(jnp.float32)
        cycle = jnp.einsum("ak,jbk->bja", amp_wide, int_wide).reshape(V, J * V)
        return (res_row.astype(jnp.float32) + cycle).astype(jnp.bfloat16)

    return lax.map(one_row, (amplitudes, occ_slab, residual))
```

```python
import functools

import jax
import jax.numpy as jnp
from jax import lax
from jax.experimental import pallas as pl
from jax.experimental.pallas import tpu as pltpu
from jax.sharding import Mesh, PartitionSpec as P

V = 1536
J = 16
TILE = 256
STEPS = (0, 3, 1, 2)
WIDTHS = (512, 768, 1536)
PLACES = (0, 1, 2)
VMEM_LIMIT = 16 * 1024 * 1024


def labels_at(position, offsets):
    total = jnp.zeros(position.shape, jnp.int32)
    for k in range(1, 8):
        total = total + (position >= offsets[k]).astype(jnp.int32)
    return total


def fold(width, rows, source, out, where, code, offsets):
    block = 32
    col = labels_at(lax.broadcasted_iota(jnp.int32, (1, V), 1), offsets)

    def step(n, carry):
        start = pl.multiple_of(n * block, block)
        here = lax.broadcasted_iota(jnp.int32, (block, 1), 0) + (where[0] + rows + start)
        want = jnp.bitwise_xor(labels_at(here, offsets), code)
        folded = None
        for left in range(0, V, width):
            size = min(width, V - left)
            cut = slice(left, left + size)
            part = source[pl.ds(rows + start, block), cut].astype(jnp.float32)
            part = jnp.where(want == col[:, cut], part, 0.0)
            if size < width:
                part = jnp.concatenate([part, jnp.zeros((block, width - size), jnp.float32)], axis=1)
            folded = part if folded is None else folded + part
        out[pl.ds(start, block), :] = folded.astype(jnp.bfloat16)
        return carry

    lax.fori_loop(0, out.shape[0] // block, step, 0)


def fold_kernel(width, where, offsets, inner, slab, outer, amps, ints, low, high, out):
    code = jnp.bitwise_xor(outer[where[1]], inner[0])
    fold(width, 0, ints, low, where, code, offsets)
    fold(width, low.shape[0], ints, high, where, code, offsets)
    code = jnp.bitwise_xor(slab[0], inner[0])
    fold(width, 0, amps, out, where, code, offsets)


def stage_kernel(source, out, sem):
    copy = pltpu.make_async_copy(source, out, sem)
    copy.start()
    copy.wait()


def flip_kernel(source, out):
    out[...] = source[...].T


def flip(amps):
    vmem = pl.BlockSpec(memory_space=pltpu.VMEM)
    return pl.pallas_call(
        flip_kernel,
        out_shape=jax.ShapeDtypeStruct(amps.shape[::-1], amps.dtype),
        in_specs=[vmem],
        out_specs=vmem,
        compiler_params=pltpu.CompilerParams(vmem_limit_bytes=VMEM_LIMIT),
        name="flip",
    )(amps)


def stage(residual):
    return pl.pallas_call(
        stage_kernel,
        out_shape=jax.ShapeDtypeStruct(residual.shape, residual.dtype),
        in_specs=[pl.BlockSpec(memory_space=pl.ANY)],
        out_specs=pl.BlockSpec(memory_space=pltpu.VMEM),
        scratch_shapes=[pltpu.SemaphoreType.DMA],
        compiler_params=pltpu.CompilerParams(vmem_limit_bytes=VMEM_LIMIT),
        name="stage",
    )(residual)


def cycle_kernel(parts, tiles, where, offsets, slab, outer, amps, *refs):
    pieces = refs[: len(parts)]
    res = refs[len(parts)]
    out_hbm, held, rows_seen, cols_seen, sem = refs[-5:]
    half = held.shape[2]
    x, z = where[2], where[3]
    rows_seen[...] = labels_at(
        where[0] + lax.broadcasted_iota(jnp.int32, rows_seen.shape, 0), offsets
    )
    cols_seen[...] = labels_at(lax.broadcasted_iota(jnp.int32, cols_seen.shape, 1), offsets)
    stores = []
    for n, (low, far) in enumerate(parts):
        own = slice(0, half) if low else slice(half, 2 * half)
        js = []
        for near in STEPS:
            dx, dz = (near, far) if low else (far, near)
            js.append(lax.rem(x + dx, 4) * 4 + lax.rem(z + dz, 4))
        wants = [
            jnp.bitwise_xor(rows_seen[own, :], jnp.bitwise_xor(slab[0], outer[j])) for j in js
        ]

        def tile(start):
            cut = pl.ds(start, TILE)
            cycle = jnp.dot(pieces[n][...], amps[:, cut], preferred_element_type=jnp.float32)
            cols = cols_seen[0:1, cut]
            for s in range(4):
                want = jnp.concatenate([wants[s]] * (TILE // 128), axis=1)
                term = jnp.where(want == cols, cycle[s * half : (s + 1) * half], 0.0)
                here = pl.ds(pl.multiple_of(js[s] * V + start, TILE), TILE)
                held[n, s, :, cut] = (res[own, here].astype(jnp.float32) + term).astype(
                    jnp.bfloat16
                )

        def group(g, carry):
            for t in range(tiles):
                tile(pl.multiple_of(g * (tiles * TILE), TILE) + t * TILE)
            return carry

        if tiles * TILE == V:
            for t in range(tiles):
                tile(t * TILE)
        else:
            lax.fori_loop(0, V // (tiles * TILE), group, 0)
        for s in range(4):
            place = own, pl.ds(pl.multiple_of(js[s] * V, V), V)
            store = pltpu.make_async_copy(held.at[n, s], out_hbm.at[place], sem.at[n, s])
            store.start()
            stores.append(store)
    for store in stores:
        store.wait()


def add_cycle(parts, scalars, amps, pieces, residual, out):
    smem = pl.BlockSpec(memory_space=pltpu.SMEM)
    vmem = pl.BlockSpec(memory_space=pltpu.VMEM)
    hbm = pl.BlockSpec(memory_space=pl.ANY)
    rows = residual.shape[0]
    width = amps.shape[0]
    half = rows // 2
    count = len(parts)
    before = () if out is None else (out,)
    operands = (*scalars, amps, *pieces, residual, *before)
    return pl.pallas_call(
        functools.partial(cycle_kernel, parts, 6 if width < V else 1),
        out_shape=jax.ShapeDtypeStruct(residual.shape, jnp.bfloat16),
        in_specs=[smem] * 4 + [vmem] * (2 + count) + [hbm] * len(before),
        out_specs=hbm,
        scratch_shapes=[
            pltpu.VMEM((count, 4, half, V), jnp.bfloat16),
            pltpu.VMEM((rows, 128), jnp.int32),
            pltpu.VMEM((8, V), jnp.int32),
            pltpu.SemaphoreType.DMA((count, 4)),
        ],
        input_output_aliases={} if out is None else {len(operands) - 1: 0},
        compiler_params=pltpu.CompilerParams(vmem_limit_bytes=VMEM_LIMIT),
        cost_estimate=pl.CostEstimate(
            flops=8 * count * half * V * width,
            bytes_accessed=16 * count * half * V,
            transcendentals=0,
        ),
        name="add_cycle",
    )(*operands)


def ring(shift):
    return [(k, (k + shift) % 4) for k in range(4)]


def neighbours(low, low_axis, high, high_axis):
    got = []
    for shift in (1, 3, 2):
        got.append(lax.ppermute(low, low_axis, ring(shift)))
        got.append(lax.ppermute(high, high_axis, ring(shift)))
    return got[0::2], got[1::2]


def branch(width, where, offsets, inner, slab, outer, amplitudes, integrals, residual):
    rows = amplitudes.shape[0]
    half = rows // 2
    smem = pl.BlockSpec(memory_space=pltpu.SMEM)
    vmem = pl.BlockSpec(memory_space=pltpu.VMEM)
    low, high, amp_folded = pl.pallas_call(
        functools.partial(fold_kernel, width),
        out_shape=[
            jax.ShapeDtypeStruct((n, width), jnp.bfloat16) for n in (half, half, rows)
        ],
        in_specs=[smem] * 5 + [vmem] * 2,
        out_specs=[vmem] * 3,
        compiler_params=pltpu.CompilerParams(vmem_limit_bytes=VMEM_LIMIT),
        name="fold",
    )(where, offsets, inner, slab, outer, amplitudes, integrals)
    amps = flip(lax.all_gather(amp_folded, ("y", "core"), axis=0, tiled=True))

    low_near, high_near = lax.optimization_barrier(neighbours(low, "x", high, "z"))
    amps, residual = lax.optimization_barrier((amps, residual))
    residual = stage(residual)
    low4 = jnp.concatenate([low, *low_near], axis=0)
    high4 = jnp.concatenate([high, *high_near], axis=0)
    low_far, high_far = neighbours(low4, "z", high4, "x")

    scalars = (where, offsets, slab, outer)
    parts = ((True, 0), (False, 0), (False, 2), (False, 1))
    pieces = (low4, high4, high_far[2], high_far[1])
    out = add_cycle(parts, scalars, amps, pieces, residual, None)
    parts = ((False, 3), (True, 2), (True, 1), (True, 3))
    pieces = (high_far[0], low_far[2], low_far[1], low_far[0])
    return add_cycle(parts, scalars, amps, pieces, residual, out)


def per_device(amplitudes, integrals, occ_slab, occ_inner, occ_outer, vir_offset, residual):
    rows = integrals.shape[1]
    x, z = lax.axis_index("x"), lax.axis_index("z")
    pair = lax.axis_index("y") * 2 + lax.axis_index("core")
    where = jnp.stack([pair * rows, x * 4 + z, x, z]).astype(jnp.int32)
    widest = jnp.max(vir_offset[1:] - vir_offset[:-1])
    order = sum((widest > w).astype(jnp.int32) for w in WIDTHS[:-1])
    choice = jnp.int32(PLACES[-1])
    for k, place in enumerate(PLACES[:-1]):
        choice = jnp.where(order == k, place, choice)
    out = lax.switch(
        choice,
        [functools.partial(branch, WIDTHS[PLACES.index(k)]) for k in range(len(WIDTHS))],
        where,
        vir_offset,
        occ_inner,
        occ_slab,
        occ_outer,
        amplitudes[0],
        integrals[0],
        residual[0],
    )
    return out[None]


def solution(mesh):
    fine = Mesh(mesh.devices.reshape(4, 2, 4, 4), ("y", "core", "x", "z"))
    block = P(("x", "z"), ("y", "core"), None)
    placed = (block, block, P(("x", "z")), P(), P(), P(), block)
    return jax.shard_map(
        per_device, mesh=fine, in_specs=placed, out_specs=block, check_vma=False
    )
```

```python
import functools

import jax
import jax.numpy as jnp
from jax import lax
from jax.experimental import pallas as pl
from jax.experimental.pallas import tpu as pltpu
from jax.sharding import Mesh, PartitionSpec as P

V = 1536
J = 16
TILE = 256
STEPS = (0, 3, 1, 2)
WIDTHS = (512, 768, 1536)
PLACES = (0, 1, 2)
VMEM_LIMIT = 24 * 1024 * 1024


def labels_at(position, offsets):
    total = jnp.zeros(position.shape, jnp.int32)
    for k in range(1, 8):
        total = total + (position >= offsets[k]).astype(jnp.int32)
    return total


def fold(width, rows, source, out, where, code, offsets):
    block = 32
    col = labels_at(lax.broadcasted_iota(jnp.int32, (1, V), 1), offsets)

    def step(n, carry):
        start = pl.multiple_of(n * block, block)
        here = lax.broadcasted_iota(jnp.int32, (block, 1), 0) + (where[0] + rows + start)
        want = jnp.bitwise_xor(labels_at(here, offsets), code)
        folded = None
        for left in range(0, V, width):
            size = min(width, V - left)
            cut = slice(left, left + size)
            part = source[pl.ds(rows + start, block), cut].astype(jnp.float32)
            part = jnp.where(want == col[:, cut], part, 0.0)
            if size < width:
                part = jnp.concatenate([part, jnp.zeros((block, width - size), jnp.float32)], axis=1)
            folded = part if folded is None else folded + part
        out[pl.ds(start, block), :] = folded.astype(jnp.bfloat16)
        return carry

    lax.fori_loop(0, out.shape[0] // block, step, 0)


def fold_kernel(width, where, offsets, inner, slab, outer, amps, ints, low, high, out):
    code = jnp.bitwise_xor(outer[where[1]], inner[0])
    fold(width, 0, ints, low, where, code, offsets)
    fold(width, low.shape[0], ints, high, where, code, offsets)
    code = jnp.bitwise_xor(slab[0], inner[0])
    fold(width, 0, amps, out, where, code, offsets)


def stage_kernel(source, out, sem):
    copy = pltpu.make_async_copy(source, out, sem)
    copy.start()
    copy.wait()


def source_columns(where, low, far):
    x, z = where[2], where[3]
    found = []
    for near in STEPS:
        dx, dz = (near, far) if low else (far, near)
        found.append(lax.rem(x + dx, 4) * 4 + lax.rem(z + dz, 4))
    return found


def jobs_of(parts, where, half):
    found = []
    for low, far in parts:
        first = 0 if low else half
        js = source_columns(where, low, far)
        places = [
            (pl.ds(first, half), pl.ds(pl.multiple_of(j * V, V), V)) for j in js
        ]
        found.append((first, js, places))
    return found


def set_labels(where, offsets, rows_seen, cols_seen):
    rows_seen[...] = labels_at(
        where[0] + lax.broadcasted_iota(jnp.int32, rows_seen.shape, 0), offsets
    )
    cols_seen[...] = labels_at(lax.broadcasted_iota(jnp.int32, cols_seen.shape, 1), offsets)


def add_piece(tiles, job, slab, outer, piece, amps, rows_seen, cols_seen, given, result):
    first, js, _ = job
    half = given.shape[1]
    rows = rows_seen[first : first + half, :]
    wants = [jnp.bitwise_xor(rows, jnp.bitwise_xor(slab[0], outer[j])) for j in js]

    def tile(start):
        cut = pl.ds(start, TILE)
        cycle = jnp.dot(piece[...], amps[:, cut], preferred_element_type=jnp.float32)
        cols = cols_seen[0:1, cut]
        for s in range(4):
            want = jnp.concatenate([wants[s]] * (TILE // 128), axis=1)
            term = jnp.where(want == cols, cycle[s * half : (s + 1) * half], 0.0)
            result[s, :, cut] = (given[s, :, cut].astype(jnp.float32) + term).astype(jnp.bfloat16)

    if tiles == V // TILE:
        for t in range(tiles):
            tile(t * TILE)
    else:

        def group(g, carry):
            for t in range(tiles):
                tile(pl.multiple_of(g * (tiles * TILE), TILE) + t * TILE)
            return carry

        lax.fori_loop(0, V // (tiles * TILE), group, 0)


def first_kernel(parts, later, tiles, where, offsets, slab, outer, *refs):
    count = len(parts)
    pieces = refs[:count]
    amps, res = refs[count : count + 2]
    out, flipped, staged, amps_in, held, rows_seen, cols_seen = refs[count + 2 : count + 9]
    sem_amps, sem_in, sem_out = refs[count + 9 :]
    half = held.shape[2]
    jobs = jobs_of(parts + later, where, half)
    loads, stores = [], []
    for n, (_, _, places) in enumerate(jobs):
        slot = held.at[n] if n < count else staged.at[n - count]
        loads.append(
            [
                pltpu.make_async_copy(res.at[place], slot.at[s], sem_in.at[n, s])
                for s, place in enumerate(places)
            ]
        )
        if n < count:
            stores.append(
                [
                    pltpu.make_async_copy(slot.at[s], out.at[place], sem_out.at[n, s])
                    for s, place in enumerate(places)
                ]
            )
    fetch = pltpu.make_async_copy(amps, amps_in, sem_amps)
    fetch.start()
    for load in loads[0] + loads[1]:
        load.start()
    set_labels(where, offsets, rows_seen, cols_seen)
    fetch.wait()
    flipped[...] = amps_in[...].T
    for n in range(count):
        for load in loads[n + 2]:
            load.start()
        for load in loads[n]:
            load.wait()
        add_piece(
            tiles, jobs[n], slab, outer, pieces[n], flipped, rows_seen, cols_seen,
            held.at[n], held.at[n],
        )
        for store in stores[n]:
            store.start()
    for load in loads[count + 2 :]:
        for copy in load:
            copy.start()
    for load in loads[count:]:
        for copy in load:
            copy.wait()
    for group in stores:
        for store in group:
            store.wait()


def second_kernel(parts, tiles, where, offsets, slab, outer, *refs):
    count = len(parts)
    pieces = refs[:count]
    amps, staged = refs[count : count + 2]
    out, held, rows_seen, cols_seen, sem = refs[-5:]
    half = held.shape[2]
    jobs = jobs_of(parts, where, half)
    set_labels(where, offsets, rows_seen, cols_seen)
    stores = []
    for n in range(count):
        add_piece(
            tiles, jobs[n], slab, outer, pieces[n], amps, rows_seen, cols_seen,
            staged.at[n], held.at[n],
        )
        for s, place in enumerate(jobs[n][2]):
            store = pltpu.make_async_copy(held.at[n, s], out.at[place], sem.at[n, s])
            store.start()
            stores.append(store)
    for store in stores:
        store.wait()


def add_cycle(parts, later, scalars, pieces, later_pieces, amps, residual):
    smem = pl.BlockSpec(memory_space=pltpu.SMEM)
    vmem = pl.BlockSpec(memory_space=pltpu.VMEM)
    hbm = pl.BlockSpec(memory_space=pl.ANY)
    rows = residual.shape[0]
    width = amps.shape[1]
    half = rows // 2
    count, rest = len(parts), len(later)
    tiles = V // TILE if width < V else 1
    params = pltpu.CompilerParams(vmem_limit_bytes=VMEM_LIMIT)
    cost = pl.CostEstimate(
        flops=8 * count * half * V * width,
        bytes_accessed=16 * count * half * V,
        transcendentals=0,
    )
    blocks, later_blocks = (count, 4, half, V), (rest, 4, half, V)
    labels = [pltpu.VMEM((rows, 128), jnp.int32), pltpu.VMEM((8, V), jnp.int32)]
    out, flipped, staged = pl.pallas_call(
        functools.partial(first_kernel, parts, later, tiles),
        out_shape=[
            jax.ShapeDtypeStruct(residual.shape, jnp.bfloat16),
            jax.ShapeDtypeStruct((width, V), jnp.bfloat16),
            jax.ShapeDtypeStruct(later_blocks, jnp.bfloat16),
        ],
        in_specs=[smem] * 4 + [vmem] * count + [hbm] * 2,
        out_specs=[hbm, vmem, vmem],
        scratch_shapes=[
            pltpu.VMEM((V, width), jnp.bfloat16),
            pltpu.VMEM(blocks, jnp.bfloat16),
            *labels,
            pltpu.SemaphoreType.DMA,
            pltpu.SemaphoreType.DMA((count + rest, 4)),
            pltpu.SemaphoreType.DMA((count, 4)),
        ],
        compiler_params=params,
        cost_estimate=cost,
        name="add_first",
    )(*scalars, *pieces, amps, residual)
    operands = (*scalars, *later_pieces, flipped, staged, out)
    return pl.pallas_call(
        functools.partial(second_kernel, later, tiles),
        out_shape=jax.ShapeDtypeStruct(residual.shape, jnp.bfloat16),
        in_specs=[smem] * 4 + [vmem] * (rest + 2) + [hbm],
        out_specs=hbm,
        scratch_shapes=[
            pltpu.VMEM(later_blocks, jnp.bfloat16),
            *labels,
            pltpu.SemaphoreType.DMA((rest, 4)),
        ],
        input_output_aliases={len(operands) - 1: 0},
        compiler_params=params,
        cost_estimate=cost,
        name="add_second",
    )(*operands)


def ring(shift):
    return [(k, (k + shift) % 4) for k in range(4)]


def neighbours(low, low_axis, high, high_axis):
    got = []
    for shift in (1, 3, 2):
        got.append(lax.ppermute(low, low_axis, ring(shift)))
        got.append(lax.ppermute(high, high_axis, ring(shift)))
    return got[0::2], got[1::2]


def branch(width, where, offsets, inner, slab, outer, amplitudes, integrals, residual):
    rows = amplitudes.shape[0]
    half = rows // 2
    smem = pl.BlockSpec(memory_space=pltpu.SMEM)
    vmem = pl.BlockSpec(memory_space=pltpu.VMEM)
    low, high, amp_folded = pl.pallas_call(
        functools.partial(fold_kernel, width),
        out_shape=[
            jax.ShapeDtypeStruct((n, width), jnp.bfloat16) for n in (half, half, rows)
        ],
        in_specs=[smem] * 5 + [vmem] * 2,
        out_specs=[vmem] * 3,
        compiler_params=pltpu.CompilerParams(vmem_limit_bytes=VMEM_LIMIT),
        name="fold",
    )(where, offsets, inner, slab, outer, amplitudes, integrals)
    copies = jnp.broadcast_to(amp_folded[None], (V // rows, rows, width))
    amps = lax.all_to_all(copies, ("y", "core"), 0, 0).reshape(V, width)

    low_near, high_near = lax.optimization_barrier(neighbours(low, "x", high, "z"))
    low4 = jnp.concatenate([low, *low_near], axis=0)
    high4 = jnp.concatenate([high, *high_near], axis=0)
    low_far, high_far = neighbours(low4, "z", high4, "x")

    scalars = (where, offsets, slab, outer)
    parts = ((True, 0), (False, 0), (False, 2))
    pieces = (low4, high4, high_far[2])
    later = ((True, 2), (True, 1), (True, 3), (False, 1), (False, 3))
    later_pieces = (low_far[2], low_far[1], low_far[0], high_far[1], high_far[0])
    return add_cycle(parts, later, scalars, pieces, later_pieces, amps, residual)


def per_device(amplitudes, integrals, occ_slab, occ_inner, occ_outer, vir_offset, residual):
    rows = integrals.shape[1]
    x, z = lax.axis_index("x"), lax.axis_index("z")
    pair = lax.axis_index("y") * 2 + lax.axis_index("core")
    where = jnp.stack([pair * rows, x * 4 + z, x, z]).astype(jnp.int32)
    widest = jnp.max(vir_offset[1:] - vir_offset[:-1])
    order = sum((widest > w).astype(jnp.int32) for w in WIDTHS[:-1])
    choice = jnp.int32(PLACES[-1])
    for k, place in enumerate(PLACES[:-1]):
        choice = jnp.where(order == k, place, choice)
    out = lax.switch(
        choice,
        [functools.partial(branch, WIDTHS[PLACES.index(k)]) for k in range(len(WIDTHS))],
        where,
        vir_offset,
        occ_inner,
        occ_slab,
        occ_outer,
        amplitudes[0],
        integrals[0],
        residual[0],
    )
    return out[None]


def solution(mesh):
    fine = Mesh(mesh.devices.reshape(4, 2, 4, 4), ("y", "core", "x", "z"))
    block = P(("x", "z"), ("y", "core"), None)
    placed = (block, block, P(("x", "z")), P(), P(), P(), block)
    return jax.shard_map(
        per_device, mesh=fine, in_specs=placed, out_specs=block, check_vma=False
    )
```

```python
import functools

import jax
import jax.numpy as jnp
from jax import lax
from jax.experimental import pallas as pl
from jax.experimental.pallas import tpu as pltpu
from jax.sharding import Mesh, PartitionSpec as P

V = 1536
J = 16
TILE = 256
STEPS = (0, 2, 1, 3)
WIDTHS = (512, 768, 1536)
PLACES = (0, 1, 2)
VMEM_LIMIT = 24 * 1024 * 1024


def labels_at(position, offsets):
    total = jnp.zeros(position.shape, jnp.int32)
    for k in range(1, 8):
        total = total + (position >= offsets[k]).astype(jnp.int32)
    return total


def fold(width, rows, source, outs, where, code, offsets):
    block = 32
    col = labels_at(lax.broadcasted_iota(jnp.int32, (1, V), 1), offsets)

    def step(n, carry):
        start = pl.multiple_of(n * block, block)
        here = lax.broadcasted_iota(jnp.int32, (block, 1), 0) + (where[0] + rows + start)
        want = jnp.bitwise_xor(labels_at(here, offsets), code)
        folded = None
        for left in range(0, V, width):
            size = min(width, V - left)
            cut = slice(left, left + size)
            part = source[pl.ds(rows + start, block), cut].astype(jnp.float32)
            part = jnp.where(want == col[:, cut], part, 0.0)
            if size < width:
                part = jnp.concatenate([part, jnp.zeros((block, width - size), jnp.float32)], axis=1)
            folded = part if folded is None else folded + part
        for target in outs:
            target[pl.ds(start, block), :] = folded.astype(jnp.bfloat16)
        return carry

    lax.fori_loop(0, outs[0].shape[0] // block, step, 0)


def fold_kernel(width, where, offsets, inner, slab, outer, amps, ints, low, high, out):
    code = jnp.bitwise_xor(outer[where[1]], inner[0])
    fold(width, 0, ints, [low], where, code, offsets)
    fold(width, low.shape[0], ints, [high], where, code, offsets)
    code = jnp.bitwise_xor(slab[0], inner[0])
    fold(width, 0, amps, [out.at[n] for n in range(out.shape[0])], where, code, offsets)


def stage_kernel(source, out, sem):
    copy = pltpu.make_async_copy(source, out, sem)
    copy.start()
    copy.wait()


def source_columns(where, low, far):
    x, z = where[2], where[3]
    found = []
    for near in STEPS:
        dx, dz = (near, far) if low else (far, near)
        found.append(lax.rem(x + dx, 4) * 4 + lax.rem(z + dz, 4))
    return found


def jobs_of(parts, where, half):
    found = []
    for low, far in parts:
        first = 0 if low else half
        js = source_columns(where, low, far)
        places = [
            (pl.ds(first, half), pl.ds(pl.multiple_of(j * V, V), V)) for j in js
        ]
        found.append((first, js, places))
    return found


def set_labels(where, offsets, rows_seen, cols_seen):
    rows_seen[...] = labels_at(
        where[0] + lax.broadcasted_iota(jnp.int32, rows_seen.shape, 0), offsets
    )
    cols_seen[...] = labels_at(lax.broadcasted_iota(jnp.int32, cols_seen.shape, 1), offsets)


def add_piece(tiles, job, slab, outer, piece, amps, rows_seen, cols_seen, given, result):
    first, js, _ = job
    half = given.shape[1]
    rows = rows_seen[first : first + half, :]
    wants = [jnp.bitwise_xor(rows, jnp.bitwise_xor(slab[0], outer[j])) for j in js]

    def tile(start):
        cut = pl.ds(start, TILE)
        cycle = jnp.dot(piece[...], amps[:, cut], preferred_element_type=jnp.float32)
        cols = cols_seen[0:1, cut]
        for s in range(4):
            want = jnp.concatenate([wants[s]] * (TILE // 128), axis=1)
            term = jnp.where(want == cols, cycle[s * half : (s + 1) * half], 0.0)
            result[s, :, cut] = (given[s, :, cut].astype(jnp.float32) + term).astype(jnp.bfloat16)

    if tiles == V // TILE:
        for t in range(tiles):
            tile(t * TILE)
    else:

        def group(g, carry):
            for t in range(tiles):
                tile(pl.multiple_of(g * (tiles * TILE), TILE) + t * TILE)
            return carry

        lax.fori_loop(0, V // (tiles * TILE), group, 0)


def first_kernel(parts, later, tiles, where, offsets, slab, outer, *refs):
    count = len(parts)
    pieces = refs[:count]
    amps, res = refs[count : count + 2]
    out, flipped, staged, amps_in, held, rows_seen, cols_seen = refs[count + 2 : count + 9]
    sem_amps, sem_in, sem_out = refs[count + 9 :]
    half = held.shape[2]
    jobs = jobs_of(parts + later, where, half)
    loads, stores = [], []
    for n, (_, _, places) in enumerate(jobs):
        slot = held.at[n] if n < count else staged.at[n - count]
        loads.append(
            [
                pltpu.make_async_copy(res.at[place], slot.at[s], sem_in.at[n, s])
                for s, place in enumerate(places)
            ]
        )
        if n < count:
            stores.append(
                [
                    pltpu.make_async_copy(slot.at[s], out.at[place], sem_out.at[n, s])
                    for s, place in enumerate(places)
                ]
            )
    fetch = pltpu.make_async_copy(amps, amps_in, sem_amps)
    fetch.start()
    for load in loads[0] + loads[1]:
        load.start()
    set_labels(where, offsets, rows_seen, cols_seen)
    fetch.wait()
    flipped[...] = amps_in[...].T
    for n in range(count):
        for load in loads[n + 2]:
            load.start()
        for load in loads[n]:
            load.wait()
        add_piece(
            tiles, jobs[n], slab, outer, pieces[n], flipped, rows_seen, cols_seen,
            held.at[n], held.at[n],
        )
        for store in stores[n]:
            store.start()
    for load in loads[count + 2 :]:
        for copy in load:
            copy.start()
    for load in loads[count:]:
        for copy in load:
            copy.wait()
    for group in stores:
        for store in group:
            store.wait()


def second_kernel(parts, tiles, where, offsets, slab, outer, *refs):
    count = len(parts)
    pieces = refs[:count]
    amps, staged = refs[count : count + 2]
    out, held, rows_seen, cols_seen, sem = refs[-5:]
    half = held.shape[2]
    jobs = jobs_of(parts, where, half)
    set_labels(where, offsets, rows_seen, cols_seen)
    stores = []
    for n in range(count):
        add_piece(
            tiles, jobs[n], slab, outer, pieces[n], amps, rows_seen, cols_seen,
            staged.at[n], held.at[n],
        )
        for s, place in enumerate(jobs[n][2]):
            store = pltpu.make_async_copy(held.at[n, s], out.at[place], sem.at[n, s])
            store.start()
            stores.append(store)
    for store in stores:
        store.wait()


def add_cycle(parts, later, scalars, pieces, later_pieces, amps, residual):
    smem = pl.BlockSpec(memory_space=pltpu.SMEM)
    vmem = pl.BlockSpec(memory_space=pltpu.VMEM)
    hbm = pl.BlockSpec(memory_space=pl.ANY)
    rows = residual.shape[0]
    width = amps.shape[1]
    half = rows // 2
    count, rest = len(parts), len(later)
    tiles = V // TILE if width < V else 1
    params = pltpu.CompilerParams(vmem_limit_bytes=VMEM_LIMIT)
    cost = pl.CostEstimate(
        flops=8 * count * half * V * width,
        bytes_accessed=16 * count * half * V,
        transcendentals=0,
    )
    blocks, later_blocks = (count, 4, half, V), (rest, 4, half, V)
    labels = [pltpu.VMEM((rows, 128), jnp.int32), pltpu.VMEM((8, V), jnp.int32)]
    out, flipped, staged = pl.pallas_call(
        functools.partial(first_kernel, parts, later, tiles),
        out_shape=[
            jax.ShapeDtypeStruct(residual.shape, jnp.bfloat16),
            jax.ShapeDtypeStruct((width, V), jnp.bfloat16),
            jax.ShapeDtypeStruct(later_blocks, jnp.bfloat16),
        ],
        in_specs=[smem] * 4 + [vmem] * count + [hbm] * 2,
        out_specs=[hbm, vmem, vmem],
        scratch_shapes=[
            pltpu.VMEM((V, width), jnp.bfloat16),
            pltpu.VMEM(blocks, jnp.bfloat16),
            *labels,
            pltpu.SemaphoreType.DMA,
            pltpu.SemaphoreType.DMA((count + rest, 4)),
            pltpu.SemaphoreType.DMA((count, 4)),
        ],
        compiler_params=params,
        cost_estimate=cost,
        name="add_first",
    )(*scalars, *pieces, amps, residual)
    operands = (*scalars, *later_pieces, flipped, staged, out)
    return pl.pallas_call(
        functools.partial(second_kernel, later, tiles),
        out_shape=jax.ShapeDtypeStruct(residual.shape, jnp.bfloat16),
        in_specs=[smem] * 4 + [vmem] * (rest + 2) + [hbm],
        out_specs=hbm,
        scratch_shapes=[
            pltpu.VMEM(later_blocks, jnp.bfloat16),
            *labels,
            pltpu.SemaphoreType.DMA((rest, 4)),
        ],
        input_output_aliases={len(operands) - 1: 0},
        compiler_params=params,
        cost_estimate=cost,
        name="add_second",
    )(*operands)


def ring(shift):
    return [(k, (k + shift) % 4) for k in range(4)]


def neighbours(low, low_axis, high, high_axis):
    got = []
    for shift in (2, 3, 1):
        got.append(lax.ppermute(low, low_axis, ring(shift)))
        got.append(lax.ppermute(high, high_axis, ring(shift)))
    return got[0::2], got[1::2]


def branch(width, where, offsets, inner, slab, outer, amplitudes, integrals, residual):
    rows = amplitudes.shape[0]
    half = rows // 2
    smem = pl.BlockSpec(memory_space=pltpu.SMEM)
    vmem = pl.BlockSpec(memory_space=pltpu.VMEM)
    low, high, copies = pl.pallas_call(
        functools.partial(fold_kernel, width),
        out_shape=[
            jax.ShapeDtypeStruct((*n, width), jnp.bfloat16)
            for n in ((half,), (half,), (V // rows, rows))
        ],
        in_specs=[smem] * 5 + [vmem] * 2,
        out_specs=[vmem] * 3,
        compiler_params=pltpu.CompilerParams(vmem_limit_bytes=VMEM_LIMIT),
        name="fold",
    )(where, offsets, inner, slab, outer, amplitudes, integrals)
    amps = lax.all_to_all(copies, ("y", "core"), 0, 0).reshape(V, width)

    low_near, high_near = lax.optimization_barrier(neighbours(low, "x", high, "z"))
    low4 = jnp.concatenate([low, *low_near], axis=0)
    high4 = jnp.concatenate([high, *high_near], axis=0)
    low_far, high_far = neighbours(low4, "z", high4, "x")

    scalars = (where, offsets, slab, outer)
    parts = ((True, 0), (False, 0), (False, 3))
    pieces = (low4, high4, high_far[2])
    later = ((False, 1), (False, 2), (True, 3), (True, 1), (True, 2))
    later_pieces = (high_far[1], high_far[0], low_far[2], low_far[1], low_far[0])
    return add_cycle(parts, later, scalars, pieces, later_pieces, amps, residual)


def per_device(amplitudes, integrals, occ_slab, occ_inner, occ_outer, vir_offset, residual):
    rows = integrals.shape[1]
    x, z = lax.axis_index("x"), lax.axis_index("z")
    pair = lax.axis_index("y") * 2 + lax.axis_index("core")
    where = jnp.stack([pair * rows, x * 4 + z, x, z]).astype(jnp.int32)
    widest = jnp.max(vir_offset[1:] - vir_offset[:-1])
    order = sum((widest > w).astype(jnp.int32) for w in WIDTHS[:-1])
    choice = jnp.int32(PLACES[-1])
    for k, place in enumerate(PLACES[:-1]):
        choice = jnp.where(order == k, place, choice)
    out = lax.switch(
        choice,
        [functools.partial(branch, WIDTHS[PLACES.index(k)]) for k in range(len(WIDTHS))],
        where,
        vir_offset,
        occ_inner,
        occ_slab,
        occ_outer,
        amplitudes[0],
        integrals[0],
        residual[0],
    )
    return out[None]


def solution(mesh):
    fine = Mesh(mesh.devices.reshape(4, 2, 4, 4), ("y", "core", "x", "z"))
    block = P(("x", "z"), ("y", "core"), None)
    placed = (block, block, P(("x", "z")), P(), P(), P(), block)
    return jax.shard_map(
        per_device, mesh=fine, in_specs=placed, out_specs=block, check_vma=False
    )
```
